32 devices in a mesh: wave: 8 (over z, x), cfd: 4 (over y, core).
Axes of the slice: x: 2, y: 2, z: 4, core: 2. Of those that a mesh axis runs over, the one named last changes fastest.
Arguments:
- phi_spec: float32 [2, 8192, 4096], P(None, ('wave', 'cfd')), may hold values from -6 to 6
- elevation: float32 [4096, 8192], P(('wave', 'cfd')), may hold values from -4 to 4
- hull_owner: int32 [128, 1], replicated, may hold values from 0 to 31; in each aligned block of 128 rows (0 to 127, 128 to 255, ...) at most 16 rows name the same one
- hull_place: int32 [128], replicated, may hold values from 0 to 1023
- cell_need: int32 [1024], P(('wave', 'cfd')), may hold values from 0 to 127
- cfd_velocity: float32 [1024, 3, 8, 128], P(('wave', 'cfd')), may hold values from -6 to 6
- relax_gain: float32 [1024], P(('wave', 'cfd')), may hold values from 0.2 to 1
Outputs:
- w_surface: float32 [4096, 8192], P(('wave', 'cfd'))
- blended: float32 [1024, 3, 8, 128], P(('wave', 'cfd'))
- pressure: float32 [1024, 8, 128], P(('wave', 'cfd'))
The draws below stay inside these ranges and needn't reach their ends.
Inputs may be any that keep to these rules, and one draw needn't show every extreme that they name: `hull_owner`: no device owns more than 16 hull-zone blocks, and one device owns exactly 16.
All inputs are finite; a program needn't handle non-finite values.
Results may differ from the reference program's by a relative error of at most 0.00011.
Values sent between devices are 32-bit elements; how exact they have to be, the bound alone decides.
A program may use at most 192 MiB of HBM per device.

```python
import math
import jax
import jax.numpy as jnp
import numpy as np
from jax import lax

NX = 8192
NY = 4096
BY = 8
TILE = 128
SWEEPS = 4
CB = 32
HB = 128
CAP = 16
TILES_DEV = 1024
N_WAVE = 8
N_CFD = 4


def set_ends(result, rng, smallest, top_value):
    place = [jax.random.randint(jax.random.fold_in(rng, axis), (), 0, length) for axis, length in enumerate(result.shape)]
    widest = result.shape.index(max(result.shape))
    next_to = place[:widest] + [(place[widest] + 1) % result.shape[widest]] + place[widest + 1:]
    return result.at[tuple(place)].set(smallest).at[tuple(next_to)].set(top_value)


def block_scale(key, dims, shards, low, high):
    def one(axis_at, blocks):
        draws = jax.random.uniform(jax.random.fold_in(jax.random.fold_in(key, 6), axis_at), (blocks,), jnp.float32, low / len(shards), high / len(shards))
        return jnp.repeat(jnp.exp(draws), dims[axis_at] // blocks).reshape((-1,) + (1,) * (len(dims) - axis_at - 1))

    level = one(*shards[0])
    for cut in shards[1:]:
        level = level * one(*cut)
    return level


def routed_block(key, own, number, rows, amount, top, bound, skew):
    order = jax.random.permutation(key, amount)
    packed, usual = load_shares(amount, rows * top, bound, skew, True), load_shares(amount, rows * top, bound, skew, False)
    places = jnp.arange(amount)

    def named(sizes, offset_by):
        used = int((sizes > 0).sum())
        fixed = max(1, used // 4)
        moved = fixed + (places - fixed + offset_by * (used - fixed)) % max(1, amount - fixed)
        return jnp.zeros((amount,), jnp.int32).at[order[jnp.where(places < fixed, places, moved)]].set(jnp.asarray(sizes, jnp.int32))

    sizes = jnp.where(number % 4 == 0, named(packed, number // 4), named(usual, number - number // 4 - 1))
    mixed = jax.random.permutation(jax.random.fold_in(own, 3), amount)
    giver, taker = mixed[0:amount // 2 * 2:2], mixed[1:amount // 2 * 2:2]
    margin = jnp.minimum(sizes[giver] - 1, bound - sizes[taker]) // 2
    margin = jnp.where((giver == order[0]) | (taker == order[0]) | (sizes[taker] == 0), 0, jnp.maximum(margin, 0))
    moved = jax.random.randint(jax.random.fold_in(own, 4), (amount // 2,), 0, 1 << 20) % (margin + 1)
    sizes = sizes.at[giver].add(-moved).at[taker].add(moved)
    labels = jnp.searchsorted(jnp.cumsum(sizes), jnp.arange(rows * top), side="right").astype(jnp.int32)
    grid = labels.reshape(top, rows).T
    grid = grid[jax.random.permutation(jax.random.fold_in(own, 1), rows)]
    offset_by = jax.random.randint(jax.random.fold_in(own, 2), (rows, 1), 0, top)
    return jnp.take_along_axis(grid, (jnp.arange(top)[None, :] + offset_by) % top, axis=1)


def load_shares(count, total, bound, skew, full):
    loads = [(1 << 20) // math.isqrt(grade ** skew) + 1 for grade in range(1, count + 1)]
    largest = bound if full else min(bound, max(-(-total // count), total * loads[0] // sum(loads)))
    least = 1 if total - largest >= count - 1 else 0
    given, spare = [largest] + [least] * (count - 1), total - largest - least * (count - 1)
    while spare > 0:
        free = [i for i in range(1, count) if given[i] < largest] or [i for i in range(1, count) if given[i] < bound]
        whole, budget = sum([loads[i] for i in free]), spare
        for i in free:
            more = min(bound - given[i], max(1, budget * loads[i] // whole), spare)
            given[i] = given[i] + more
            spare = spare - more
    return np.array(given)


def scatter_about(key, shape, deviation, most, pieces=(), kind=jnp.bfloat16):
    array = deviation * jax.random.normal(key, shape, jnp.float32)
    if pieces:
        array = array * block_scale(key, shape, pieces, -0.22, 0.18)
    return jnp.clip(array, -most, most).astype(kind)


def setup_inputs(seed: int = 0) -> dict:
    streams_of = jax.random.split(jax.random.key(seed), 8)
    phi_spec = scatter_about(streams_of[0], (2, NX, NY), 0.4, 6.0, ((1, 32),), jnp.float32)
    elevation = scatter_about(streams_of[1], (NY, NX), 0.3, 4.0, ((0, 32),), jnp.float32)
    hull_owner_keys = jax.random.split(jax.random.fold_in(streams_of[2], 1), HB // HB)
    hull_owner_turns = jax.random.permutation(jax.random.fold_in(streams_of[2], 3), HB // HB)
    hull_owner = jax.vmap(lambda own, number: routed_block(jax.random.fold_in(streams_of[2], 2), own, number, HB, N_WAVE * N_CFD, 1, CAP, 2))(hull_owner_keys, hull_owner_turns).reshape((HB, 1))
    hull_place = set_ends(jax.random.randint(streams_of[3], (HB,), 0, TILES_DEV), jax.random.fold_in(streams_of[3], 1), 0, TILES_DEV - 1).astype(jnp.int32)
    cell_need = set_ends(jax.random.randint(streams_of[4], (N_WAVE * N_CFD * CB,), 0, HB), jax.random.fold_in(streams_of[4], 1), 0, HB - 1).astype(jnp.int32)
    cfd_velocity = scatter_about(streams_of[5], (N_WAVE * N_CFD * CB, 3, BY, TILE), 1.0, 6.0, ((0, 32),), jnp.float32)
    relax_gain = jnp.clip(0.2 + 0.8 * jax.random.uniform(streams_of[6], (N_WAVE * N_CFD * CB,), jnp.float32) ** block_scale(streams_of[6], (N_WAVE * N_CFD * CB,), ((0, 32),), -0.2, 0.2), 0.2, 1.0)
    return {"phi_spec": phi_spec, "elevation": elevation, "hull_owner": hull_owner, "hull_place": hull_place, "cell_need": cell_need, "cfd_velocity": cfd_velocity, "relax_gain": relax_gain}


def wave_numbers(start, count, length):
    signed = (start + jnp.arange(count, dtype=jnp.int32) + length // 2) % length - length // 2
    return signed.astype(jnp.float32) * (2.0 * math.pi / length)

def blend_smooth(hos_blocks, cfd_velocity, relax_gain):
    position = jnp.arange(TILE, dtype=jnp.float32)
    ramp = 1.0 - (position + 0.5) / TILE
    weight = relax_gain[:, None, None, None] * ramp[None, None, None, :]
    blended = weight * hos_blocks + (1.0 - weight) * cfd_velocity
    padded_u = jnp.pad(blended[:, 0], ((0, 0), (0, 0), (1, 1)))
    padded_v = jnp.pad(blended[:, 1], ((0, 0), (1, 1), (0, 0)))
    source = (padded_u[:, :, 2:] - padded_u[:, :, :-2]) * 0.5 + (padded_v[:, 2:, :] - padded_v[:, :-2, :]) * 0.5
    pressure = jnp.zeros_like(source)
    for sweep in range(SWEEPS):
        padded = jnp.pad(pressure, ((0, 0), (1, 1), (1, 1)))
        beside = padded[:, 2:, 1:-1] + padded[:, :-2, 1:-1] + padded[:, 1:-1, 2:] + padded[:, 1:-1, :-2]
        pressure = (beside - source) / 4.5
    return (blended, pressure)

def reference(phi_spec, elevation, hull_owner, hull_place, cell_need, cfd_velocity, relax_gain):
    spectrum = phi_spec[0] + 1j * phi_spec[1]
    wave_x = wave_numbers(0, NX, NX)[:, None]
    wave_y = wave_numbers(0, NY, NY)[None, :]
    magnitude = jnp.sqrt(wave_x * wave_x + wave_y * wave_y)

    def backward(values):
        return jnp.real(jnp.fft.ifft2(values, norm='ortho')).T
    w_first = backward(magnitude * spectrum)
    curvature = backward(magnitude * magnitude * spectrum)
    vel_x = backward(1j * wave_x * spectrum)
    vel_y = backward(1j * wave_y * spectrum)
    product = -elevation * w_first
    transformed = jnp.fft.fft2(product.T, norm='ortho')
    w_second = backward(magnitude * transformed)
    w_surface = w_first + w_second + elevation * curvature
    kinematics = jnp.stack([vel_x, vel_y, w_surface])
    lines_dev = NY // (N_WAVE * N_CFD)
    across = NX // TILE
    owners = hull_owner[:, 0].astype(jnp.int32)
    chosen = cell_need.astype(jnp.int32)
    places = hull_place.astype(jnp.int32)[chosen]
    line_start = (owners[chosen] * lines_dev + places // across * BY).astype(jnp.int32)
    point_start = (places % across * TILE).astype(jnp.int32)

    def cut(line_at, point_at):
        return lax.dynamic_slice(kinematics, (jnp.int32(0), line_at, point_at), (3, BY, TILE))
    hos_blocks = jax.vmap(cut)(line_start, point_start)
    blended, pressure = blend_smooth(hos_blocks, cfd_velocity, relax_gain)
    return (w_surface, blended, pressure)
```

```python
import math

import jax
import jax.numpy as jnp
import numpy as np
from jax import lax
from jax.experimental import pallas as pl
from jax.experimental.pallas import tpu as pltpu
from jax.sharding import PartitionSpec as P

YA = 32
BY = 8
TILE = 128
SWEEPS = 4
HULL_DEV = 4


HIGHEST = lax.Precision.HIGHEST


def wave_numbers(start, count, length):
    signed = (start + jnp.arange(count, dtype=jnp.int32) + length // 2) % length - length // 2
    return signed.astype(jnp.float32) * (2.0 * math.pi / length)


def phase_table(rows, cols, length, sign):
    product = (
        jnp.arange(rows, dtype=jnp.int32)[:, None]
        * jnp.arange(cols, dtype=jnp.int32)[None, :]
        % length
    )
    angle = product.astype(jnp.float32) * (2.0 * math.pi / length)
    return (jnp.cos(angle), sign * jnp.sin(angle))


def complex_einsum(formula, table_re, table_im, data_re, data_im, real_only):
    direct = jnp.einsum(formula, table_re, data_re, precision=HIGHEST)
    crossed = jnp.einsum(formula, table_im, data_im, precision=HIGHEST)
    if real_only:
        return direct - crossed
    mixed_one = jnp.einsum(formula, table_re, data_im, precision=HIGHEST)
    mixed_two = jnp.einsum(formula, table_im, data_re, precision=HIGHEST)
    return (direct - crossed, mixed_one + mixed_two)


def rotate(values_re, values_im, factor_re, factor_im):
    return (
        values_re * factor_re - values_im * factor_im,
        values_re * factor_im + values_im * factor_re,
    )


def lines_inverse(spectra_re, spectra_im, devices):
    count, rows_x, span_y = spectra_re.shape
    first = YA
    second = span_y // first
    shaped_re = spectra_re.reshape(count, rows_x, first, second)
    shaped_im = spectra_im.reshape(count, rows_x, first, second)
    one_re, one_im = phase_table(first, first, first, 1.0)
    turn_re, turn_im = phase_table(first, second, span_y, 1.0)
    two_re, two_im = phase_table(second, second, second, 1.0)
    section_re, section_im = complex_einsum(
        "kn,frnm->frkm", one_re, one_im, shaped_re, shaped_im, False
    )
    section_re, section_im = rotate(section_re, section_im, turn_re, turn_im)
    final_re, final_im = complex_einsum(
        "qm,frkm->fqkr", two_re, two_im, section_re, section_im, False
    )
    scaling = 1.0 / math.sqrt(span_y)
    return (
        (final_re * scaling).reshape(count, devices, -1),
        (final_im * scaling).reshape(count, devices, -1),
    )


def columns_inverse(blocks_re, blocks_im, rows_y, span_x):
    count, devices, merged = blocks_re.shape
    rows_x = merged // rows_y
    shaped_re = blocks_re.reshape(count, devices, rows_y, rows_x)
    shaped_im = blocks_im.reshape(count, devices, rows_y, rows_x)
    one_re, one_im = phase_table(devices, devices, devices, 1.0)
    turn_re, turn_im = phase_table(devices, rows_x, span_x, 1.0)
    two_re, two_im = phase_table(rows_x, rows_x, rows_x, 1.0)
    section_re, section_im = complex_einsum(
        "kj,fjyr->fkyr", one_re, one_im, shaped_re, shaped_im, False
    )
    section_re, section_im = rotate(
        section_re, section_im, turn_re[:, None, :], turn_im[:, None, :]
    )
    final = complex_einsum("qr,fkyr->fyqk", two_re, two_im, section_re, section_im, True)
    return final.reshape(count, rows_y, span_x) * (1.0 / math.sqrt(span_x))


def lines_transform(data_re, data_im, sign):
    span_y, rows_x = data_re.shape
    first = YA
    second = span_y // first
    shaped_re = data_re.reshape(first, second, rows_x)
    shaped_im = data_im.reshape(first, second, rows_x)
    one_re, one_im = phase_table(first, first, first, sign)
    turn_re, turn_im = phase_table(first, second, span_y, sign)
    two_re, two_im = phase_table(second, second, second, sign)
    section_re, section_im = complex_einsum(
        "kn,nmr->kmr", one_re, one_im, shaped_re, shaped_im, False
    )
    section_re, section_im = rotate(
        section_re, section_im, turn_re[:, :, None], turn_im[:, :, None]
    )
    final_re, final_im = complex_einsum(
        "qm,kmr->qkr", two_re, two_im, section_re, section_im, False
    )
    scaling = 1.0 / math.sqrt(span_y)
    return (
        (final_re * scaling).reshape(span_y, rows_x),
        (final_im * scaling).reshape(span_y, rows_x),
    )


def blend_smooth(hos_blocks, cfd_velocity, relax_gain):
    position = jnp.arange(TILE, dtype=jnp.float32)
    ramp = 1.0 - (position + 0.5) / TILE
    weight = relax_gain[:, None, None, None] * ramp[None, None, None, :]
    blended = weight * hos_blocks + (1.0 - weight) * cfd_velocity
    padded_u = jnp.pad(blended[:, 0], ((0, 0), (0, 0), (1, 1)))
    padded_v = jnp.pad(blended[:, 1], ((0, 0), (1, 1), (0, 0)))
    source = (padded_u[:, :, 2:] - padded_u[:, :, :-2]) * 0.5 + (
        padded_v[:, 2:, :] - padded_v[:, :-2, :]
    ) * 0.5
    pressure = jnp.zeros_like(source)
    for sweep in range(SWEEPS):
        padded = jnp.pad(pressure, ((0, 0), (1, 1), (1, 1)))
        beside = (
            padded[:, 2:, 1:-1] + padded[:, :-2, 1:-1] + padded[:, 1:-1, 2:] + padded[:, 1:-1, :-2]
        )
        pressure = (beside - source) / 4.5
    return (blended, pressure)


def local_general(phi_spec, elevation, hull_owner, hull_place, cell_need, cfd_velocity, relax_gain):
    devices = lax.axis_size(("wave", "cfd"))
    rank_here = lax.axis_index(("wave", "cfd"))
    rows_x = phi_spec.shape[1]
    span_y = phi_spec.shape[2]
    rows_y, span_x = elevation.shape
    wave_x = wave_numbers(rank_here * rows_x, rows_x, span_x)[:, None]
    wave_y = wave_numbers(0, span_y, span_y)[None, :]
    magnitude = jnp.sqrt(wave_x * wave_x + wave_y * wave_y)
    spec_re = phi_spec[0]
    spec_im = phi_spec[1]
    fields_re = jnp.stack(
        [magnitude * spec_re, magnitude * magnitude * spec_re, -wave_x * spec_im, -wave_y * spec_im]
    )
    fields_im = jnp.stack(
        [magnitude * spec_im, magnitude * magnitude * spec_im, wave_x * spec_re, wave_y * spec_re]
    )
    lines_re, lines_im = lines_inverse(fields_re, fields_im, devices)
    moved_re, moved_im = (
        lax.all_to_all(lines_re, ("wave", "cfd"), split_axis=1, concat_axis=1, tiled=True),
        lax.all_to_all(lines_im, ("wave", "cfd"), split_axis=1, concat_axis=1, tiled=True),
    )
    physical = columns_inverse(moved_re, moved_im, rows_y, span_x)
    w_first = physical[0]
    curvature = physical[1]
    vel_x = physical[2]
    vel_y = physical[3]
    product = -elevation * w_first
    shaped = product.reshape(rows_y, rows_x, devices)
    one_re, one_im = phase_table(rows_x, rows_x, rows_x, -1.0)
    turn_re, turn_im = phase_table(rows_x, devices, span_x, -1.0)
    two_re, two_im = phase_table(devices, devices, devices, -1.0)
    section_re = jnp.einsum("kn,ynm->ykm", one_re, shaped, precision=HIGHEST)
    section_im = jnp.einsum("kn,ynm->ykm", one_im, shaped, precision=HIGHEST)
    section_re, section_im = rotate(section_re, section_im, turn_re, turn_im)
    final_re, final_im = complex_einsum(
        "qm,ykm->qyk", two_re, two_im, section_re, section_im, False
    )
    scaling = 1.0 / math.sqrt(span_x)
    sent_re = (final_re * scaling).reshape(devices, -1)
    sent_im = (final_im * scaling).reshape(devices, -1)
    got_re, got_im = (
        lax.all_to_all(sent_re, ("wave", "cfd"), split_axis=0, concat_axis=0, tiled=True),
        lax.all_to_all(sent_im, ("wave", "cfd"), split_axis=0, concat_axis=0, tiled=True),
    )
    lines_re, lines_im = lines_transform(
        got_re.reshape(span_y, rows_x), got_im.reshape(span_y, rows_x), -1.0
    )
    wave_row = wave_numbers(rank_here * rows_x, rows_x, span_x)[None, :]
    wave_col = wave_numbers(0, span_y, span_y)[:, None]
    magnitude_lines = jnp.sqrt(wave_row * wave_row + wave_col * wave_col)
    back_re, back_im = lines_transform(lines_re * magnitude_lines, lines_im * magnitude_lines, 1.0)
    return_re, return_im = (
        lax.all_to_all(
            back_re.reshape(devices, -1), ("wave", "cfd"), split_axis=0, concat_axis=0, tiled=True
        ),
        lax.all_to_all(
            back_im.reshape(devices, -1), ("wave", "cfd"), split_axis=0, concat_axis=0, tiled=True
        ),
    )
    w_second = columns_inverse(return_re[None], return_im[None], rows_y, span_x)[0]
    w_surface = w_first + w_second + elevation * curvature
    kinematics = jnp.stack([vel_x, vel_y, w_surface])
    across = span_x // TILE

    def cut(place):
        line_at = place // across * BY
        point_at = place % across * TILE
        return lax.dynamic_slice(kinematics, (jnp.int32(0), line_at, point_at), (3, BY, TILE))

    owners = hull_owner[:, 0]
    owner_table = (owners[:, None] == jnp.arange(devices, dtype=jnp.int32)[None, :]).astype(
        jnp.int32
    )
    owner_rank = jnp.sum(jnp.cumsum(owner_table, axis=0) * owner_table, axis=1) - 1
    mine = owners == rank_here
    capacity = 4 * HULL_DEV
    select = (
        mine[None, :] & (owner_rank[None, :] == jnp.arange(capacity, dtype=jnp.int32)[:, None])
    ).astype(jnp.int32)
    slot_place = jnp.sum(select * hull_place[None, :], axis=1)
    slot_valid = jnp.sum(select, axis=1).astype(jnp.float32)
    tiles = jax.vmap(cut)(slot_place) * slot_valid[:, None, None, None]
    gathered = lax.all_gather(tiles, ("wave", "cfd"), axis=0, tiled=True)
    slot_index = owners[cell_need] * capacity + owner_rank[cell_need]
    hos_blocks = jnp.take(gathered, slot_index, axis=0)
    blended, pressure = blend_smooth(hos_blocks, cfd_velocity, relax_gain)
    return (w_surface, blended, pressure)


YS = 16
LANES = 128
VMEM_BYTES = 56 * 1024 * 1024


def slab_dft(values, sign):
    count = len(values)
    if count == 1:
        return values
    even = slab_dft(values[0::2], sign)
    odd = slab_dft(values[1::2], sign)
    half = count // 2
    low, high = [], []
    for k in range(half):
        even_re, even_im = even[k]
        odd_re, odd_im = odd[k]
        if k == 0:
            turned_re, turned_im = odd_re, odd_im
        elif 4 * k == count:
            turned_re, turned_im = (-odd_im, odd_re) if sign > 0 else (odd_im, -odd_re)
        elif 8 * k == count or 8 * k == 3 * count:
            root = math.sqrt(0.5)
            cos = root if 8 * k == count else -root
            turned_re = odd_re * cos - odd_im * (sign * root)
            turned_im = odd_im * cos + odd_re * (sign * root)
        else:
            cos = math.cos(2.0 * math.pi * k / count)
            sin = sign * math.sin(2.0 * math.pi * k / count)
            turned_re = odd_re * cos - odd_im * sin
            turned_im = odd_re * sin + odd_im * cos
        low.append((even_re + turned_re, even_im + turned_im))
        high.append((even_re - turned_re, even_im - turned_im))
    return low + high


def phases(rows, cols, length, sign, scale=1.0):
    product = np.arange(rows)[:, None] * np.arange(cols)[None, :] % length
    angle = product * (2.0 * math.pi / length)
    return np.cos(angle) * scale, sign * np.sin(angle) * scale


def two_parts(table):
    table = np.asarray(table, np.float32)
    high = table.astype(jnp.bfloat16)
    rest = (table - high.astype(np.float32)).astype(jnp.bfloat16)
    return jnp.asarray(np.stack([high, rest]))


def left_table(count, sign, scale):
    cos, sin = phases(count, count, count, sign, scale)
    return two_parts(np.block([[cos, -sin], [sin, cos]]))


def right_table(count, sign, scale, real_only):
    cos, sin = phases(count, count, count, sign, scale)
    if real_only:
        return two_parts(np.concatenate([cos, -sin], axis=0))
    return two_parts(np.block([[cos, sin], [-sin, cos]]))


def split(value):
    high = value.astype(jnp.bfloat16)
    return high, (value - high.astype(jnp.float32)).astype(jnp.bfloat16)


def multiply(left, right, dims):
    def one(a, b):
        return lax.dot_general(a, b, (dims, ((), ())), preferred_element_type=jnp.float32)

    return one(left[0], right[0]) + (one(left[0], right[1]) + one(left[1], right[0]))


PLAIN = ((1,), (0,))
ACROSS = ((1,), (1,))


def rows_kernel(quantity, span_x, phi_ref, wx_ref, turn_ref, table_ref, out_ref, work_ref):
    lines = phi_ref.shape[1]
    span_y = phi_ref.shape[2]
    long = span_y // YS

    def first(i, carry):
        rows = pl.ds(pl.multiple_of(i * 8, 8), 8)
        for lane in range(0, long, LANES):
            values = []
            for n in range(YS):
                at = n * long + lane
                re = phi_ref[0, rows, at : at + LANES]
                im = phi_ref[1, rows, at : at + LANES]
                if quantity != "potential":
                    place = lax.broadcasted_iota(jnp.int32, (8, LANES), 1) + (
                        at - (span_y if n >= YS // 2 else 0)
                    )
                    wy = place.astype(jnp.float32) * (2.0 * math.pi / span_y)
                    if quantity == "vertical":
                        wx = wx_ref[rows, :]
                        factor = jnp.sqrt(wx * wx + wy * wy)
                        re, im = re * factor, im * factor
                    else:
                        re, im = -(wy * im), wy * re
                values.append((re, im))
            for k, (re, im) in enumerate(slab_dft(values, 1.0)):
                cos = turn_ref[0, k : k + 1, lane : lane + LANES]
                sin = turn_ref[1, k : k + 1, lane : lane + LANES]
                re, im = rotate(re, im, cos, sin)
                work_ref[k, rows, lane : lane + LANES] = re
                work_ref[k, rows, long + lane : long + lane + LANES] = im
        return carry

    lax.fori_loop(0, lines // 8, first, 0)

    def second(k, carry):
        done = multiply((table_ref[0], table_ref[1]), split(work_ref[k]), ACROSS)
        out_ref[:, 0, k] = done[:long].reshape(long // 8, 8, lines)
        out_ref[:, 1, k] = done[long:].reshape(long // 8, 8, lines)
        return carry

    lax.fori_loop(0, YS, second, 0)


def rows_inverse(phi_spec, wx_wide, quantity, span_x):
    _, rows_x, span_y = phi_spec.shape
    long = span_y // YS
    cos, sin = phases(YS, long, span_y, 1.0)
    turn = jnp.asarray(np.stack([cos, sin]), jnp.float32)
    table = left_table(long, 1.0, 1.0 / math.sqrt(span_y))

    def kernel(*refs):
        rows_kernel(quantity, span_x, *refs)

    return pl.pallas_call(
        kernel,
        grid=(rows_x // LANES,),
        in_specs=[
            pl.BlockSpec((2, LANES, span_y), lambda i: (0, i, 0)),
            pl.BlockSpec((LANES, LANES), lambda i: (i, 0)),
            pl.BlockSpec(turn.shape, lambda i: (0, 0, 0)),
            pl.BlockSpec(table.shape, lambda i: (0, 0, 0)),
        ],
        out_specs=pl.BlockSpec((long // 8, 2, YS, 8, LANES), lambda i: (0, 0, 0, 0, i)),
        out_shape=jax.ShapeDtypeStruct((long // 8, 2, YS, 8, rows_x), jnp.float32),
        scratch_shapes=[pltpu.VMEM((YS, LANES, 2 * long), jnp.float32)],
        compiler_params=pltpu.CompilerParams(vmem_limit_bytes=VMEM_BYTES),
        cost_estimate=pl.CostEstimate(
            flops=4 * 10**10, bytes_accessed=4 * rows_x * span_y * 4, transcendentals=0
        ),
        name="rows_" + quantity,
    )(phi_spec, wx_wide, turn, table)


def points_inverse(got_ref, turn_ref, work_ref):
    devices, _, lines, long = got_ref.shape
    for row in range(0, lines, 8):
        rows = slice(row, row + 8)

        def one(i, carry):
            lane = pl.multiple_of(i * LANES, LANES)
            here = pl.ds(lane, LANES)
            values = [
                (got_ref[s, 0, rows, here], got_ref[s, 1, rows, here]) for s in range(devices)
            ]
            for k, (re, im) in enumerate(slab_dft(values, 1.0)):
                re, im = rotate(re, im, turn_ref[0, k : k + 1, here], turn_ref[1, k : k + 1, here])
                work_ref[k, rows, here] = re
                work_ref[k, rows, pl.ds(lane + long, LANES)] = im
            return carry

        lax.fori_loop(0, long // LANES, one, 0)


def first_order_kernel(
    got_ref, elev_ref, turn_ref, real_ref, table_ref, first_ref, out_ref, work_ref
):
    devices, _, lines, long = got_ref.shape
    points_inverse(got_ref, turn_ref, work_ref)
    flat = work_ref[...].reshape(devices * lines, 2 * long)
    w_first = multiply(split(flat), (real_ref[0], real_ref[1]), PLAIN)
    first_ref[...] = w_first.reshape(devices, lines, long)
    product = -elev_ref[...].reshape(devices * lines, long) * w_first
    pair = jnp.concatenate([product, w_first], axis=1)
    done = multiply(split(pair), (table_ref[0], table_ref[1]), PLAIN)
    work_ref[...] = done.reshape(devices, lines, 2 * long)
    for row in range(0, lines, 8):
        rows = slice(row, row + 8)

        def one(i, carry):
            lane = pl.multiple_of(i * LANES, LANES)
            here = pl.ds(lane, LANES)
            values = []
            for k in range(devices):
                re = work_ref[k, rows, here]
                im = work_ref[k, rows, pl.ds(lane + long, LANES)]
                values.append(
                    rotate(re, im, turn_ref[0, k : k + 1, here], -turn_ref[1, k : k + 1, here])
                )
            for s, (re, im) in enumerate(slab_dft(values, -1.0)):
                out_ref[s, 0, rows, here] = re
                out_ref[s, 1, rows, here] = im
            return carry

        lax.fori_loop(0, long // LANES, one, 0)


def second_order_kernel(got_ref, elev_ref, first_ref, turn_ref, table_ref, out_ref, work_ref):
    devices, _, lines, long = got_ref.shape
    points_inverse(got_ref, turn_ref, work_ref)
    flat = work_ref[...].reshape(devices * lines, 2 * long)
    done = multiply(split(flat), (table_ref[0], table_ref[1]), PLAIN)
    w_second = done[:, :long].reshape(devices, lines, long)
    curvature = done[:, long:].reshape(devices, lines, long)
    out_ref[...] = first_ref[...] + w_second + elev_ref[...] * curvature


LINES_STEP = 16


def points_call(kernel, got, others, tables, outs, name):
    devices, _, lines, long = got.shape
    real_block = pl.BlockSpec((devices, LINES_STEP, long), lambda i: (0, i, 0))
    pair_block = pl.BlockSpec((devices, 2, LINES_STEP, long), lambda i: (0, 0, i, 0))
    blocks = {"real": real_block, "pair": pair_block}
    shapes = {"real": (devices, lines, long), "pair": (devices, 2, lines, long)}
    return pl.pallas_call(
        kernel,
        grid=(lines // LINES_STEP,),
        in_specs=[pair_block]
        + [real_block] * len(others)
        + [pl.BlockSpec(table.shape, lambda i: (0, 0, 0)) for table in tables],
        out_specs=[blocks[kind] for kind in outs],
        out_shape=[jax.ShapeDtypeStruct(shapes[kind], jnp.float32) for kind in outs],
        scratch_shapes=[pltpu.VMEM((devices, LINES_STEP, 2 * long), jnp.float32)],
        compiler_params=pltpu.CompilerParams(vmem_limit_bytes=VMEM_BYTES),
        cost_estimate=pl.CostEstimate(
            flops=2 * 10**10, bytes_accessed=5 * got.size * 2, transcendentals=0
        ),
        name=name,
    )(got, *others, *tables)


def filter_kernel(got_ref, wx_ref, turn_ref, forward_ref, back_ref, out_ref, work_ref):
    parts = got_ref.shape[0]
    long = parts * 8
    span_y = long * YS

    def one(k, carry):
        pair = jnp.concatenate(
            [got_ref[:, 0, k].reshape(long, LANES), got_ref[:, 1, k].reshape(long, LANES)], axis=0
        )
        work_ref[k] = multiply((forward_ref[0], forward_ref[1]), split(pair), PLAIN)
        return carry

    lax.fori_loop(0, YS, one, 0)

    def two(i, carry):
        at = pl.multiple_of(i * 8, 8)
        rows = pl.ds(at, 8)
        below = pl.ds(at + long, 8)
        wx = wx_ref[...]
        wx_square = wx * wx
        values = []
        for k in range(YS):
            values.append(
                rotate(
                    work_ref[k, rows, :],
                    work_ref[k, below, :],
                    turn_ref[0, k, rows, :],
                    -turn_ref[1, k, rows, :],
                )
            )
        values = slab_dft(values, -1.0)
        for n in range(YS):
            place = (
                lax.broadcasted_iota(jnp.int32, (8, LANES), 0)
                + at
                + (n * long - (span_y if n >= YS // 2 else 0))
            )
            wy = place.astype(jnp.float32) * (2.0 * math.pi / span_y)
            magnitude = jnp.sqrt(wx_square + wy * wy)
            values[n] = (values[n][0] * magnitude, values[n][1] * magnitude)
        for k, (re, im) in enumerate(slab_dft(values, 1.0)):
            re, im = rotate(re, im, turn_ref[0, k, rows, :], turn_ref[1, k, rows, :])
            work_ref[k, rows, :] = re
            work_ref[k, below, :] = im
        return carry

    lax.fori_loop(0, long // 8, two, 0)

    def three(k, carry):
        done = multiply((back_ref[0], back_ref[1]), split(work_ref[k]), PLAIN)
        out_ref[:, 0, k] = done[:long].reshape(parts, 8, LANES)
        out_ref[:, 1, k] = done[long:].reshape(parts, 8, LANES)
        return carry

    lax.fori_loop(0, YS, three, 0)


def filter_lines(got, wx_row):
    parts, _, _, _, rows_x = got.shape
    long = parts * 8
    span_y = long * YS
    cos, sin = phases(YS, long, span_y, 1.0)
    turn = jnp.broadcast_to(
        jnp.asarray(np.stack([cos, sin]), jnp.float32)[..., None], (2, YS, long, LANES)
    )
    forward = left_table(long, -1.0, 1.0 / math.sqrt(span_y))
    back = left_table(long, 1.0, 1.0 / math.sqrt(span_y))
    block = pl.BlockSpec((parts, 2, YS, 8, LANES), lambda i: (0, 0, 0, 0, i))
    return pl.pallas_call(
        filter_kernel,
        grid=(rows_x // LANES,),
        in_specs=[
            block,
            pl.BlockSpec((8, LANES), lambda i: (0, i)),
            pl.BlockSpec(turn.shape, lambda i: (0, 0, 0, 0)),
            pl.BlockSpec(forward.shape, lambda i: (0, 0, 0)),
            pl.BlockSpec(back.shape, lambda i: (0, 0, 0)),
        ],
        out_specs=block,
        out_shape=jax.ShapeDtypeStruct(got.shape, jnp.float32),
        scratch_shapes=[pltpu.VMEM((YS, 2 * long, LANES), jnp.float32)],
        compiler_params=pltpu.CompilerParams(vmem_limit_bytes=VMEM_BYTES),
        name="filter_lines",
    )(got, wx_row, turn, forward, back)


def exchange(values):
    return lax.all_to_all(values, ("wave", "cfd"), split_axis=0, concat_axis=0, tiled=True)


def cut_tiles(grid_values, places):
    across = grid_values.shape[1] // TILE

    def kernel(place_ref, in_ref, out_ref):
        out_ref[0] = in_ref[...]

    return pl.pallas_call(
        kernel,
        grid_spec=pltpu.PrefetchScalarGridSpec(
            num_scalar_prefetch=1,
            grid=(places.shape[0],),
            in_specs=[
                pl.BlockSpec((BY, TILE), lambda i, place: (place[i] // across, place[i] % across))
            ],
            out_specs=pl.BlockSpec((1, BY, TILE), lambda i, place: (i, 0, 0)),
        ),
        out_shape=jax.ShapeDtypeStruct((places.shape[0], BY, TILE), jnp.float32),
        name="cut_tiles",
    )(places, grid_values)


def blend_kernel(slot_ref, need_ref, gain_ref, upper_ref, level_ref, cfd_ref, out_ref, press_ref):
    lane = lax.broadcasted_iota(jnp.int32, (BY, TILE), 1)
    line = lax.broadcasted_iota(jnp.int32, (BY, TILE), 0)
    ramp = 1.0 - (lane.astype(jnp.float32) + 0.5) / TILE

    def later(value):
        return jnp.where(lane == TILE - 1, 0.0, pltpu.roll(value, TILE - 1, 1))

    def before(value):
        return jnp.where(lane == 0, 0.0, pltpu.roll(value, 1, 1))

    def below(value):
        return jnp.where(line == BY - 1, 0.0, pltpu.roll(value, BY - 1, 0))

    def above(value):
        return jnp.where(line == 0, 0.0, pltpu.roll(value, 1, 0))

    def one(b, carry):
        weight = gain_ref[b] * ramp
        parts = [level_ref[0, need_ref[b]], level_ref[1, need_ref[b]], upper_ref[slot_ref[b]]]
        mixed = []
        for c in range(3):
            value = weight * parts[c] + (1.0 - weight) * cfd_ref[b, c]
            out_ref[b, c] = value
            mixed.append(value)
        u, v = mixed[0], mixed[1]
        source = (later(u) - before(u)) * 0.5 + (below(v) - above(v)) * 0.5
        pressure = jnp.zeros_like(source)
        for sweep in range(SWEEPS):
            beside = below(pressure) + above(pressure) + later(pressure) + before(pressure)
            pressure = (beside - source) / 4.5
        press_ref[b] = pressure
        return carry

    lax.fori_loop(0, cfd_ref.shape[0], one, 0)


def blend_cells(slot_index, cell_need, relax_gain, upper, level, cfd_velocity):
    scalar = pl.BlockSpec(memory_space=pltpu.SMEM)
    vector = pl.BlockSpec(memory_space=pltpu.VMEM)
    return pl.pallas_call(
        blend_kernel,
        in_specs=[scalar] * 3 + [vector] * 3,
        out_specs=[vector] * 2,
        out_shape=[
            jax.ShapeDtypeStruct(cfd_velocity.shape, jnp.float32),
            jax.ShapeDtypeStruct((cfd_velocity.shape[0], BY, TILE), jnp.float32),
        ],
        compiler_params=pltpu.CompilerParams(vmem_limit_bytes=VMEM_BYTES),
        name="blend_cells",
    )(slot_index, cell_need, relax_gain, upper, level, cfd_velocity)


def hull_velocity(spectra, hull_line, hull_point, kx, wave_x, span_x):
    count = hull_line.shape[0]
    rows_x = kx.shape[0]
    lines = hull_line[:, None] + jnp.arange(BY, dtype=jnp.int32)[None, :]
    owner, within = lines // (8 * YS), lines % (8 * YS)
    inner = within % YS * 8 + within // YS
    re_row = (owner * 2) * (8 * YS) + inner
    rows = jnp.stack([re_row, re_row + 8 * YS]).reshape(-1)

    def picked(values):
        taken = jnp.take(values.reshape(-1, rows_x), rows, axis=0)
        taken = taken.reshape(2, count, BY, rows_x)
        return taken[0], taken[1]

    potential_re, potential_im = picked(spectra[0])
    across_re, across_im = picked(spectra[1])
    along_re, along_im = -wave_x * potential_im, wave_x * potential_re
    field_re = jnp.stack([along_re, across_re])
    field_im = jnp.stack([along_im, across_im])

    def angle(point):
        turns = point[:, None] * kx[None, :] % span_x
        return turns.astype(jnp.float32) * (2.0 * math.pi / span_x)

    start = angle(hull_point)[:, None, :]
    field_re, field_im = rotate(field_re, field_im, jnp.cos(start), jnp.sin(start))
    inside = angle(jnp.arange(TILE, dtype=jnp.int32))
    scaling = 1.0 / math.sqrt(span_x)
    table = jnp.concatenate([jnp.cos(inside), -jnp.sin(inside)], axis=1) * scaling
    both = jnp.concatenate([field_re, field_im], axis=-1)
    return jnp.einsum("fhjr,tr->fhjt", both, table, precision=HIGHEST)


def local_fast(phi_spec, elevation, hull_owner, hull_place, cell_need, cfd_velocity, relax_gain):
    devices = lax.axis_size(("wave", "cfd"))
    rank_here = lax.axis_index(("wave", "cfd"))
    rows_x = phi_spec.shape[1]
    rows_y, span_x = elevation.shape
    wave_x = wave_numbers(rank_here * rows_x, rows_x, span_x)
    wx_wide = jnp.broadcast_to(wave_x[:, None], (rows_x, LANES))
    wx_row = jnp.broadcast_to(wave_x[None, :], (8, rows_x))

    sent = rows_inverse(phi_spec, wx_wide, "vertical", span_x)
    sent, wx_after = lax.optimization_barrier((sent, wx_wide))
    got = exchange(sent)

    potential = rows_inverse(phi_spec, wx_after, "potential", span_x)
    across = rows_inverse(phi_spec, wx_after, "across", span_x)
    owners = hull_owner[:, 0]
    hull_blocks = span_x // TILE
    hull_line = owners * rows_y + hull_place // hull_blocks * BY
    hull_point = hull_place % hull_blocks * TILE
    kx = rank_here * rows_x + jnp.arange(rows_x, dtype=jnp.int32)
    level = hull_velocity((potential, across), hull_line, hull_point, kx, wave_x, span_x)
    got, level = lax.optimization_barrier((got, level))
    level = lax.psum(level, ("wave", "cfd"))

    elev = elevation.reshape(8, YS, rows_x, devices).transpose(3, 1, 0, 2)
    elev = elev.reshape(devices, rows_y, rows_x)

    cos, sin = phases(devices, rows_x, span_x, 1.0)
    turn = jnp.asarray(np.stack([cos, sin]), jnp.float32)
    scaling = 1.0 / math.sqrt(span_x)
    real_table = right_table(rows_x, 1.0, scaling, True)
    forward_table = right_table(rows_x, -1.0, scaling, False)
    back_table = right_table(rows_x, 1.0, scaling, False)

    w_first, paired = points_call(
        first_order_kernel,
        got.reshape(devices, 2, rows_y, rows_x),
        [elev],
        [turn, real_table, forward_table],
        ["real", "pair"],
        "first_order",
    )
    returned = exchange(paired).reshape(devices, 2, YS, 8, rows_x)
    filtered = exchange(filter_lines(returned, wx_row))
    (surface,) = points_call(
        second_order_kernel,
        filtered.reshape(devices, 2, rows_y, rows_x),
        [elev, w_first],
        [turn, back_table],
        ["real"],
        "second_order",
    )
    w_surface = surface.reshape(devices, YS, 8, rows_x).transpose(2, 1, 3, 0)
    w_surface = w_surface.reshape(rows_y, span_x)

    owner_table = (owners[:, None] == jnp.arange(devices, dtype=jnp.int32)[None, :]).astype(
        jnp.int32
    )
    owner_rank = jnp.sum(jnp.cumsum(owner_table, axis=0) * owner_table, axis=1) - 1
    mine = owners == rank_here
    capacity = 4 * HULL_DEV
    select = (
        mine[None, :] & (owner_rank[None, :] == jnp.arange(capacity, dtype=jnp.int32)[:, None])
    ).astype(jnp.int32)
    slot_place = jnp.sum(select * hull_place[None, :], axis=1)
    tiles = cut_tiles(w_surface, slot_place)
    gathered = lax.all_gather(tiles, ("wave", "cfd"), axis=0, tiled=True)
    slot_index = owners[cell_need] * capacity + owner_rank[cell_need]
    blended, pressure = blend_cells(
        slot_index, cell_need, relax_gain, gathered, level, cfd_velocity
    )
    return (w_surface, blended, pressure)


def local(phi_spec, elevation, *others):
    devices = lax.axis_size(("wave", "cfd"))
    rows_x, span_y = phi_spec.shape[1:]
    fits = (
        devices <= 32
        and elevation.shape[0] == 8 * YS
        and rows_x % LANES == 0
        and span_y // YS % LANES == 0
    )
    return (local_fast if fits else local_general)(phi_spec, elevation, *others)


def solution(mesh):
    return jax.shard_map(
        local,
        mesh=mesh,
        in_specs=(
            P(None, ("wave", "cfd"), None),
            P(("wave", "cfd"), None),
            P(),
            P(),
            P(("wave", "cfd")),
            P(("wave", "cfd"), None, None, None),
            P(("wave", "cfd")),
        ),
        out_specs=(
            P(("wave", "cfd"), None),
            P(("wave", "cfd"), None, None, None),
            P(("wave", "cfd"), None, None),
        ),
        check_vma=False,
    )
```
